32 devices in a mesh: sec: 2 (over x), shot: 8 (over z, core), win: 2 (over y).
Axes of the slice: x: 2, y: 2, z: 4, core: 2. Of those that a mesh axis runs over, the one named last changes fastest.
Arguments:
- shot_rows: bfloat16 [512, 4, 2, 4096], P('shot'), may hold values from -6 to 6
- aperture: int32 [512, 4], P('shot'), may hold values from 0 to 7, all different within a row; in each aligned block of 64 rows (0 to 63, 64 to 127, ...) at most 64 rows name the same one
- panel: bfloat16 [8, 2, 4096, 4096], P('shot', None, None, ('sec', 'win')), may hold values from -0.09375 to 0.09375
- recorded: bfloat16 [512, 2, 4096], P('shot', None, ('sec', 'win')), may hold values from -6 to 6
- shift: int32 [512], P('shot'), may hold values from 0 to 16
Outputs:
- predicted: float32 [512, 2, 4096], P('shot', None, ('sec', 'win'))
- primaries: float32 [512, 2, 4096], P('shot', None, ('sec', 'win'))
The draws below stay inside these ranges and needn't reach their ends.
Inputs may be any that keep to these rules, and one draw needn't show every extreme that they name: `aperture`: each shot names 4 different panels. Among the 64 shots of one index of shot, no panel is named by more than 64 entries, a bound that some block reaches.
All inputs are finite; a program needn't handle non-finite values.
Results may differ from the reference program's by a relative error of at most 0.0003.
Values may be sent and summed in bfloat16 or wider, within the bound.
No kernel may reach another device: no remote copies, remote signals or barrier semaphores. Data moves between devices by JAX's collectives and lax.ppermute only.
A program may use at most 128 MiB of HBM per device.

```python
import math
import jax
import jax.numpy as jnp
import numpy as np
from jax import lax

KP = 4096
RECV = 4096
TAPS = 31
WL = 256
LAG = 8
APER = 4
S_DEV = 64
SHOTS = 512
CAP = 64
N_SHOT = 8


def with_ends(result, key, least, largest):
    dims = result.shape
    place = [jax.random.randint(jax.random.fold_in(key, axis), (), 0, dims[axis]) for axis in range(len(dims))]
    result = result.at[tuple(place)].set(least)
    longest = dims.index(max(dims))
    place[longest] = (place[longest] + 1) % dims[longest]
    return result.at[tuple(place)].set(largest)


def steps_of(key, dims, pieces, least, top_value):
    def one(axis_at, blocks):
        steps = jax.random.uniform(jax.random.fold_in(jax.random.fold_in(key, 6), axis_at), (blocks,), jnp.float32, least / len(pieces), top_value / len(pieces))
        return jnp.repeat(jnp.exp(steps), dims[axis_at] // blocks).reshape((-1,) + (1,) * (len(dims) - axis_at - 1))

    factor_of = one(*pieces[0])
    for cut in pieces[1:]:
        factor_of = factor_of * one(*cut)
    return factor_of


def routed_block(rng, own, number, rows, number_of, top, most, skew):
    order = jax.random.permutation(rng, number_of)
    packed, common = shares(number_of, rows * top, most, skew, True), shares(number_of, rows * top, most, skew, False)
    places = jnp.arange(number_of)

    def named(lengths, rotation):
        used = int((lengths > 0).sum())
        fixed = max(1, used // 4)
        passed = fixed + (places - fixed + rotation * (used - fixed)) % max(1, number_of - fixed)
        return jnp.zeros((number_of,), jnp.int32).at[order[jnp.where(places < fixed, places, passed)]].set(jnp.asarray(lengths, jnp.int32))

    lengths = jnp.where(number % 4 == 0, named(packed, number // 4), named(common, number - number // 4 - 1))
    mixed = jax.random.permutation(jax.random.fold_in(own, 3), number_of)
    donor, sink = mixed[0:number_of // 2 * 2:2], mixed[1:number_of // 2 * 2:2]
    slack = jnp.minimum(lengths[donor] - 1, most - lengths[sink]) // 2
    slack = jnp.where((donor == order[0]) | (sink == order[0]) | (lengths[sink] == 0), 0, jnp.maximum(slack, 0))
    passed = jax.random.randint(jax.random.fold_in(own, 4), (number_of // 2,), 0, 1 << 20) % (slack + 1)
    lengths = lengths.at[donor].add(-passed).at[sink].add(passed)
    members = jnp.searchsorted(jnp.cumsum(lengths), jnp.arange(rows * top), side="right").astype(jnp.int32)
    listing = members.reshape(top, rows).T
    listing = listing[jax.random.permutation(jax.random.fold_in(own, 1), rows)]
    rotation = jax.random.randint(jax.random.fold_in(own, 2), (rows, 1), 0, top)
    return jnp.take_along_axis(listing, (jnp.arange(top)[None, :] + rotation) % top, axis=1)


def shares(amount, total, most, skew, full):
    weights = [(1 << 20) // math.isqrt(rank ** skew) + 1 for rank in range(1, amount + 1)]
    largest = most if full else min(most, max(-(-total // amount), total * weights[0] // sum(weights)))
    least = 1 if total - largest >= amount - 1 else 0
    given, surplus = [largest] + [least] * (amount - 1), total - largest - least * (amount - 1)
    while surplus > 0:
        candidates = [i for i in range(1, amount) if given[i] < largest] or [i for i in range(1, amount) if given[i] < most]
        whole, budget = sum([weights[i] for i in candidates]), surplus
        for i in candidates:
            extra = min(most - given[i], max(1, budget * weights[i] // whole), surplus)
            given[i] = given[i] + extra
            surplus = surplus - extra
    return np.array(given)


def gaussian(key, dims, width, reach, cuts=(), held_as=jnp.bfloat16):
    values = width * jax.random.normal(key, dims, jnp.float32)
    if cuts:
        values = values * steps_of(key, dims, cuts, -0.22, 0.18)
    return jnp.clip(values, -reach, reach).astype(held_as)


def setup_inputs(seed: int = 0) -> dict:
    seeds = jax.random.split(jax.random.key(seed), 6)
    shot_rows = gaussian(seeds[0], (SHOTS, APER, 2, KP), 1.0, 6.0, ((0, 8),))
    aperture_keys = jax.random.split(jax.random.fold_in(seeds[1], 1), SHOTS // S_DEV)
    aperture_turns = jax.random.permutation(jax.random.fold_in(seeds[1], 3), SHOTS // S_DEV)
    aperture = jax.vmap(lambda own, number: routed_block(jax.random.fold_in(seeds[1], 2), own, number, S_DEV, N_SHOT, APER, CAP, 2))(aperture_keys, aperture_turns).reshape((SHOTS, APER))
    panel = gaussian(seeds[2], (N_SHOT, 2, KP, RECV), KP ** -0.5, 0.09375, ((0, 8), (3, 4)))
    recorded = gaussian(seeds[3], (SHOTS, 2, RECV), 1.0, 6.0, ((0, 8), (2, 4)))
    shift = with_ends(jax.random.randint(seeds[4], (SHOTS,), 0, 2 * LAG + 1), jax.random.fold_in(seeds[4], 1), 0, 2 * LAG).astype(jnp.int32)
    return {"shot_rows": shot_rows, "aperture": aperture, "panel": panel, "recorded": recorded, "shift": shift}


def complex_rows(rows_here, weights):
    parts = jnp.einsum('mck,dkr->mcdr', rows_here, weights, precision=lax.Precision.HIGHEST)
    real_part = parts[:, 0, 0] - parts[:, 1, 1]
    imag_part = parts[:, 0, 1] + parts[:, 1, 0]
    return jnp.stack([real_part, imag_part], axis=1)

def reference(shot_rows, aperture, panel, recorded, shift):
    limit = 2 * S_DEV * APER
    rows_flat = shot_rows.reshape(SHOTS * APER, 2, KP)
    ap_flat = aperture.reshape(SHOTS * APER)

    def add_panel(total, index):
        hits = ap_flat == index
        chosen = jnp.nonzero(hits, size=limit, fill_value=0)[0].astype(jnp.int32)
        live = (jnp.arange(limit, dtype=jnp.int32) < jnp.sum(hits.astype(jnp.int32))).astype(jnp.float32)
        rows_here = rows_flat[chosen].astype(jnp.float32)
        weights = lax.dynamic_index_in_dim(panel, index, 0, keepdims=False).astype(jnp.float32)
        terms = complex_rows(rows_here, weights) * live[:, None, None]
        return (total.at[chosen // APER].add(terms), None)
    start_sum = jnp.zeros((SHOTS, 2, RECV), jnp.float32)
    predicted = lax.scan(add_panel, start_sum, jnp.arange(N_SHOT, dtype=jnp.int32))[0]
    edge = (TAPS - 1) // 2 + LAG
    windows = RECV // WL

    def fit_shot(item):
        row, record, begin = item
        padded = jnp.pad(row, ((0, 0), (edge, edge)))
        aligned = lax.dynamic_slice_in_dim(padded, begin.astype(jnp.int32), RECV + TAPS - 1, 1)
        columns = jnp.stack([aligned[:, j:j + RECV] for j in range(TAPS)], axis=1)
        design = columns.reshape(2, TAPS, windows, WL)
        target = record.astype(jnp.float32).reshape(2, windows, WL)
        gram = jnp.einsum('cjwt,ckwt->wjk', design, design, precision=lax.Precision.HIGHEST)
        gram = gram + 1.0 * jnp.eye(TAPS, dtype=jnp.float32)
        moment = jnp.einsum('cjwt,cwt->wj', design, target, precision=lax.Precision.HIGHEST)
        factor = jnp.linalg.cholesky(gram)
        filters = jax.scipy.linalg.cho_solve((factor, True), moment[..., None])[..., 0]
        matched = jnp.einsum('wj,cjwt->cwt', filters, design, precision=lax.Precision.HIGHEST)
        return (target - matched).reshape(2, RECV)
    primaries = lax.map(fit_shot, (predicted, recorded, shift))
    return (predicted, primaries)
```

```python
import jax
import jax.numpy as jnp
from jax import lax
from jax.experimental import pallas as pl
from jax.experimental.pallas import tpu as pltpu
from jax.sharding import PartitionSpec as P

TAPS = 31
WL = 256
LAG = 8
EDGE = (TAPS - 1) // 2 + LAG
LANES = 128
HALF = WL // 2


def fit_kernel(low_ref, main_ref, high_ref, rec_ref, shift_ref, out_ref, piece, ext, raw, tgt, gram, res):
    comps, shots, width = main_ref.shape
    windows = width // WL
    span = 3 * LANES
    rows = comps * windows
    half_lanes = LANES // 2

    def block_of(c, b):
        if b == 0:
            return low_ref[c]
        if b == width // LANES + 1:
            return high_ref[c]
        return main_ref[c, :, (b - 1) * LANES : b * LANES]

    for c in range(comps):
        blocks = [block_of(c, b) for b in range(width // LANES + 2)]
        turned = [
            jnp.concatenate([blocks[b], blocks[b + 1]], axis=0).T for b in range(width // LANES + 1)
        ]
        for w in range(windows):
            g = c * windows + w
            for b in range(3):
                base = g * span + b * LANES
                piece[base : base + LANES, :] = turned[2 * w + b]
            pair = jnp.concatenate(
                [
                    rec_ref[c, :, w * WL : w * WL + HALF],
                    rec_ref[c, :, w * WL + HALF : (w + 1) * WL],
                ],
                axis=0,
            ).astype(jnp.float32)
            tgt[g * HALF : (g + 1) * HALF, :] = pair.T

    first = LANES - EDGE
    need = HALF + TAPS - 1
    top = need + 2 * LAG
    lag_of = jnp.broadcast_to(shift_ref[...], (rows, LANES))

    for i in range(top):
        raw[i] = piece[pl.ds(first + i, rows, stride=span), :]
    bit = [(lag_of & (1 << n)) != 0 for n in range(5)]
    count = need + 14
    for i in range(count):
        ext[i] = jnp.where(bit[0], raw[i + 1], raw[i])
    for n in range(1, 4):
        count -= 1 << n
        for i in range(count):
            ext[i] = jnp.where(bit[n], ext[i + (1 << n)], ext[i])
    for i in range(need):
        ext[i] = jnp.where(bit[4], raw[i + 16], ext[i])

    def total(v):
        v = v + pltpu.roll(v, rows // 2, 0)
        return v + pltpu.roll(v, half_lanes, 1)

    zero = jnp.zeros((rows, LANES), jnp.float32)
    unroll = 2

    def core(step, acc):
        i = TAPS - 1 + step * unroll
        vals = [ext[i + n] for n in range(TAPS + unroll - 1)]
        for n in range(unroll):
            acc = tuple(acc[d] + vals[n] * vals[n + d] for d in range(TAPS))
        return acc

    cores = lax.fori_loop(0, (HALF - TAPS + 1) // unroll, core, (zero,) * TAPS)
    for d in range(TAPS):
        last = TAPS - 1 - d
        run = cores[d]
        heads = [None] * (last + 1)
        if last == TAPS - 1:
            heads[last] = run
        for i in range(TAPS - 2, -1, -1):
            run = run + ext[i] * ext[i + d]
            if i <= last:
                heads[i] = run
        tail = zero
        for j in range(last + 1):
            if j > 0:
                tail = tail + ext[HALF + j - 1] * ext[HALF + j - 1 + d]
            value = total(heads[j] + tail)
            gram[j, j + d] = value + 1.0 if d == 0 else value

    def moments(step, acc):
        i = step * unroll
        vals = [ext[i + n] for n in range(TAPS + unroll - 1)]
        for n in range(unroll):
            row = tgt[pl.ds(i + n, rows, stride=HALF), :]
            acc = tuple(acc[j] + row * vals[n + j] for j in range(TAPS))
        return acc

    sums = lax.fori_loop(0, HALF // unroll, moments, (zero,) * TAPS)
    for j in range(TAPS):
        gram[j, TAPS] = total(sums[j])

    inverse = []
    for col in range(TAPS):
        rows_here = tuple(gram[col, r] for r in range(col, TAPS + 1))
        if col:

            def reduce(k, acc, col=col):
                mult = gram[k, col] * res[k]
                return tuple(acc[r - col] - mult * gram[k, r] for r in range(col, TAPS + 1))

            rows_here = lax.fori_loop(0, col, reduce, rows_here)
        for r in range(col, TAPS + 1):
            gram[col, r] = rows_here[r - col]
        res[col] = 1.0 / rows_here[0]

    left = [gram[k, TAPS] for k in range(TAPS)]
    taps = [None] * TAPS
    for r in range(TAPS - 1, -1, -1):
        taps[r] = left[r] * res[r]
        for k in range(r):
            left[k] = left[k] - gram[k, r] * taps[r]

    def subtract(step, carry):
        i = step * unroll
        vals = [ext[i + n] for n in range(TAPS + unroll - 1)]
        for n in range(unroll):
            value = tgt[pl.ds(i + n, rows, stride=HALF), :]
            fit = [zero, zero, zero, zero]
            for j in range(TAPS):
                fit[j % 4] = fit[j % 4] + carry[j] * vals[n + j]
            value = value - ((fit[0] + fit[1]) + (fit[2] + fit[3]))
            tgt[pl.ds(i + n, rows, stride=HALF), :] = value
        return carry

    lax.fori_loop(0, HALF // unroll, subtract, tuple(taps))
    for c in range(comps):
        for w in range(windows):
            g = c * windows + w
            both = tgt[g * HALF : (g + 1) * HALF, :].T
            out_ref[c, :, w * WL : w * WL + HALF] = both[:half_lanes]
            out_ref[c, :, w * WL + HALF : (w + 1) * WL] = both[half_lanes:]


def fit(low, main, high, rec, shift):
    comps, shots, width = main.shape
    rows = comps * (width // WL)
    span = 3 * LANES
    top = HALF + TAPS - 1 + 2 * LAG
    lanes_shift = jnp.tile(shift, LANES // shots)[None, :]
    vec = lambda n: pltpu.VMEM((n, rows, LANES), jnp.float32)
    return pl.pallas_call(
        fit_kernel,
        out_shape=jax.ShapeDtypeStruct(main.shape, jnp.float32),
        in_specs=[pl.BlockSpec(memory_space=pltpu.VMEM)] * 5,
        out_specs=pl.BlockSpec(memory_space=pltpu.VMEM),
        scratch_shapes=[
            pltpu.VMEM((rows * span, LANES), jnp.float32),
            vec(top),
            vec(top),
            pltpu.VMEM((rows * HALF, LANES), jnp.float32),
            pltpu.VMEM((TAPS, TAPS + 1, rows, LANES), jnp.float32),
            vec(TAPS),
        ],
        compiler_params=pltpu.CompilerParams(vmem_limit_bytes=32 * 1024 * 1024),
    )(low, main, high, rec, lanes_shift)


def product_kernel(order_ref, *refs):
    pieces = refs[:-4]
    panel_ref, out_ref, by_real, by_imag = refs[-4:]
    groups, comps, shots, width = out_ref.shape
    step = pl.program_id(1)
    real, imag = panel_ref[0], panel_ref[1]

    @pl.when(step == 0)
    def _():
        by_real[...] = jnp.zeros_like(by_real)
        by_imag[...] = jnp.zeros_like(by_imag)

    for n, piece in enumerate(pieces):

        @pl.when(step == n)
        def _(piece=piece):
            rows = piece[...].reshape(groups * comps * shots, piece.shape[-1])
            by_real[...] += jnp.dot(rows, real, preferred_element_type=jnp.float32)
            by_imag[...] += jnp.dot(rows, imag, preferred_element_type=jnp.float32)

    @pl.when(step == pl.num_programs(1) - 1)
    def _():
        for g in range(groups):
            at = 2 * g * shots
            out_ref[g, 0] = by_real[at : at + shots] - by_imag[at + shots : at + 2 * shots]
            out_ref[g, 1] = by_imag[at : at + shots] + by_real[at + shots : at + 2 * shots]


def products(pieces, order, panel):
    groups, comps, shots, depth = pieces[0].shape
    width = panel.shape[3]
    tile = width // 2
    rows = groups * comps * shots
    grid_spec = pltpu.PrefetchScalarGridSpec(
        num_scalar_prefetch=1,
        grid=(width // tile, len(pieces)),
        in_specs=[pl.BlockSpec(pieces[0].shape, lambda n, k, o: (0, 0, 0, 0))] * len(pieces)
        + [pl.BlockSpec((None, 2, depth, tile), lambda n, k, o: (0, 0, o[k], n))],
        out_specs=pl.BlockSpec((groups, comps, shots, tile), lambda n, k, o: (0, 0, 0, n)),
        scratch_shapes=[pltpu.VMEM((rows, tile), jnp.float32)] * 2,
    )
    return pl.pallas_call(
        product_kernel,
        grid_spec=grid_spec,
        out_shape=jax.ShapeDtypeStruct((groups, comps, shots, width), jnp.float32),
        compiler_params=pltpu.CompilerParams(vmem_limit_bytes=48 * 1024 * 1024),
        cost_estimate=pl.CostEstimate(
            flops=4 * rows * depth * len(pieces) * width,
            bytes_accessed=4 * depth * len(pieces) * width,
            transcendentals=0,
        ),
    )(order, *pieces, panel)


def predict_dense(shot_rows, aperture, panel):
    panel_count = lax.axis_size("shot")
    parts = lax.axis_size("sec") * lax.axis_size("win")
    depth = shot_rows.shape[3] // parts
    part = lax.axis_index("sec") * lax.axis_size("win") + lax.axis_index("win")
    mine = lax.dynamic_slice_in_dim(shot_rows, part * depth, depth, 3)
    mine = mine.transpose(1, 2, 0, 3)
    named = aperture.T[None] == jnp.arange(panel_count, dtype=jnp.int32)[:, None, None]
    outgoing = jnp.zeros((panel_count,) + mine.shape[1:], mine.dtype)
    for a in range(mine.shape[0]):
        outgoing = jnp.where(named[:, a, None, :, None], mine[a][None], outgoing)
    own = lax.all_to_all(outgoing, "shot", split_axis=0, concat_axis=0, tiled=True)
    swap = [(0, 1), (1, 0)]
    half = panel_count // 2
    by_sec = lax.ppermute(own, "sec", swap)
    by_win = lax.ppermute(own, "win", swap)
    both = jnp.concatenate(
        [lax.ppermute(by_sec[:half], "win", swap), lax.ppermute(by_win[half:], "sec", swap)], axis=0
    )
    order = jnp.bitwise_xor(part, jnp.array([0, 1, 2, 3], jnp.int32)).astype(jnp.int32)
    terms = products((own, by_win, by_sec, both), order, panel)
    return lax.psum_scatter(terms, "shot", scatter_dimension=0, tiled=True)[0]


def predict_slots(shot_rows, aperture, panel, capacity):
    shot_count, slot_count = aperture.shape
    row_count = shot_count * slot_count
    trace_width = shot_rows.shape[3]
    recv_width = panel.shape[3]
    panel_count = lax.axis_size("shot")
    weights = panel[0]
    ap_flat = aperture.reshape(row_count)
    indicator = (ap_flat[:, None] == jnp.arange(panel_count, dtype=jnp.int32)[None, :]).astype(
        jnp.int32
    )
    earlier = jnp.cumsum(indicator, axis=0) - indicator
    position = jnp.sum(earlier * indicator, axis=1)
    slot_id = ap_flat * capacity + position
    source = (
        jnp.zeros((panel_count * capacity,), jnp.int32)
        .at[slot_id]
        .set(jnp.arange(row_count, dtype=jnp.int32))
    )
    rows_flat = shot_rows.reshape(row_count, 2, trace_width)
    outgoing = rows_flat[source].reshape(panel_count, capacity, 2, trace_width)
    received = lax.all_to_all(outgoing, "shot", split_axis=0, concat_axis=0, tiled=True)
    stacked = received.reshape(panel_count * capacity, 2, trace_width)
    parts = jnp.einsum("mck,dkr->mcdr", stacked, weights, preferred_element_type=jnp.float32)
    real_part = parts[:, 0, 0] - parts[:, 1, 1]
    imag_part = parts[:, 0, 1] + parts[:, 1, 0]
    terms = jnp.stack([real_part, imag_part], axis=1)
    terms = terms.reshape(panel_count, capacity, 2, recv_width)
    returned = lax.all_to_all(terms, "shot", split_axis=0, concat_axis=0, tiled=True)
    back_flat = returned.reshape(panel_count * capacity, 2, recv_width)
    predicted = jnp.sum(back_flat[slot_id].reshape(shot_count, slot_count, 2, recv_width), axis=1)
    return predicted.transpose(1, 0, 2)


def body(shot_rows, aperture, panel, recorded, shift):
    shot_count, slot_count = aperture.shape
    capacity = 2 * shot_count * slot_count // lax.axis_size("shot")
    if capacity >= shot_count:
        predicted = predict_dense(shot_rows, aperture, panel)
    else:
        predicted = predict_slots(shot_rows, aperture, panel, capacity)
    count = lax.axis_size(("sec", "win"))
    forward = [(i, i + 1) for i in range(count - 1)]
    backward = [(target, source) for source, target in forward]
    low = lax.ppermute(predicted[:, :, -LANES:], ("sec", "win"), forward)
    high = lax.ppermute(predicted[:, :, :LANES], ("sec", "win"), backward)
    primaries = fit(low, predicted, high, recorded.transpose(1, 0, 2), shift)
    return (predicted.transpose(1, 0, 2), primaries.transpose(1, 0, 2))


def solution(mesh):
    in_specs = (
        P("shot", None, None, None),
        P("shot", None),
        P("shot", None, None, ("sec", "win")),
        P("shot", None, ("sec", "win")),
        P("shot"),
    )
    out_specs = (P("shot", None, ("sec", "win")), P("shot", None, ("sec", "win")))
    return jax.shard_map(body, mesh=mesh, in_specs=in_specs, out_specs=out_specs, check_vma=False)
```

```python
import functools

import jax
import jax.numpy as jnp
from jax import lax
from jax.experimental import pallas as pl
from jax.experimental.pallas import tpu as pltpu
from jax.sharding import PartitionSpec as P

TAPS = 31
WL = 256
LAG = 8
EDGE = (TAPS - 1) // 2 + LAG
LANES = 128
HALF = WL // 2


def fit_kernel(low_ref, main_ref, high_ref, rec_ref, shift_ref, out_ref, piece, ext, raw, tgt, gram, res):
    comps, shots, width = main_ref.shape
    windows = width // WL
    span = 3 * LANES
    rows = comps * windows
    half_lanes = LANES // 2

    def block_of(c, b):
        if b == 0:
            return low_ref[c]
        if b == width // LANES + 1:
            return high_ref[c]
        return main_ref[c, :, (b - 1) * LANES : b * LANES]

    for c in range(comps):
        blocks = [block_of(c, b) for b in range(width // LANES + 2)]
        turned = [
            jnp.concatenate([blocks[b], blocks[b + 1]], axis=0).T for b in range(width // LANES + 1)
        ]
        for w in range(windows):
            g = c * windows + w
            for b in range(3):
                base = g * span + b * LANES
                piece[base : base + LANES, :] = turned[2 * w + b]
            pair = jnp.concatenate(
                [
                    rec_ref[c, :, w * WL : w * WL + HALF],
                    rec_ref[c, :, w * WL + HALF : (w + 1) * WL],
                ],
                axis=0,
            ).astype(jnp.float32)
            tgt[g * HALF : (g + 1) * HALF, :] = pair.T

    first = LANES - EDGE
    need = HALF + TAPS - 1
    top = need + 2 * LAG
    lag_of = jnp.broadcast_to(shift_ref[...], (rows, LANES))

    for i in range(top):
        raw[i] = piece[pl.ds(first + i, rows, stride=span), :]
    bit = [(lag_of & (1 << n)) != 0 for n in range(5)]
    count = need + 14
    for i in range(count):
        ext[i] = jnp.where(bit[0], raw[i + 1], raw[i])
    for n in range(1, 4):
        count -= 1 << n
        for i in range(count):
            ext[i] = jnp.where(bit[n], ext[i + (1 << n)], ext[i])
    for i in range(need):
        ext[i] = jnp.where(bit[4], raw[i + 16], ext[i])

    def total(v):
        v = v + pltpu.roll(v, rows // 2, 0)
        return v + pltpu.roll(v, half_lanes, 1)

    zero = jnp.zeros((rows, LANES), jnp.float32)
    unroll = 2

    def core(step, acc):
        i = TAPS - 1 + step * unroll
        vals = [ext[i + n] for n in range(TAPS + unroll - 1)]
        for n in range(unroll):
            acc = tuple(acc[d] + vals[n] * vals[n + d] for d in range(TAPS))
        return acc

    cores = lax.fori_loop(0, (HALF - TAPS + 1) // unroll, core, (zero,) * TAPS)
    for d in range(TAPS):
        last = TAPS - 1 - d
        run = cores[d]
        heads = [None] * (last + 1)
        if last == TAPS - 1:
            heads[last] = run
        for i in range(TAPS - 2, -1, -1):
            run = run + ext[i] * ext[i + d]
            if i <= last:
                heads[i] = run
        tail = zero
        for j in range(last + 1):
            if j > 0:
                tail = tail + ext[HALF + j - 1] * ext[HALF + j - 1 + d]
            value = total(heads[j] + tail)
            gram[j, j + d] = value + 1.0 if d == 0 else value

    def moments(step, acc):
        i = step * unroll
        vals = [ext[i + n] for n in range(TAPS + unroll - 1)]
        for n in range(unroll):
            row = tgt[pl.ds(i + n, rows, stride=HALF), :]
            acc = tuple(acc[j] + row * vals[n + j] for j in range(TAPS))
        return acc

    sums = lax.fori_loop(0, HALF // unroll, moments, (zero,) * TAPS)
    for j in range(TAPS):
        gram[j, TAPS] = total(sums[j])

    inverse = []
    for col in range(TAPS):
        rows_here = tuple(gram[col, r] for r in range(col, TAPS + 1))
        if col:

            def reduce(k, acc, col=col):
                mult = gram[k, col] * res[k]
                return tuple(acc[r - col] - mult * gram[k, r] for r in range(col, TAPS + 1))

            rows_here = lax.fori_loop(0, col, reduce, rows_here)
        for r in range(col, TAPS + 1):
            gram[col, r] = rows_here[r - col]
        res[col] = 1.0 / rows_here[0]

    left = [gram[k, TAPS] for k in range(TAPS)]
    taps = [None] * TAPS
    for r in range(TAPS - 1, -1, -1):
        taps[r] = left[r] * res[r]
        for k in range(r):
            left[k] = left[k] - gram[k, r] * taps[r]

    def subtract(step, carry):
        i = step * unroll
        vals = [ext[i + n] for n in range(TAPS + unroll - 1)]
        for n in range(unroll):
            value = tgt[pl.ds(i + n, rows, stride=HALF), :]
            fit = [zero, zero, zero, zero]
            for j in range(TAPS):
                fit[j % 4] = fit[j % 4] + carry[j] * vals[n + j]
            value = value - ((fit[0] + fit[1]) + (fit[2] + fit[3]))
            tgt[pl.ds(i + n, rows, stride=HALF), :] = value
        return carry

    lax.fori_loop(0, HALF // unroll, subtract, tuple(taps))
    for c in range(comps):
        for w in range(windows):
            g = c * windows + w
            both = tgt[g * HALF : (g + 1) * HALF, :].T
            out_ref[c, :, w * WL : w * WL + HALF] = both[:half_lanes]
            out_ref[c, :, w * WL + HALF : (w + 1) * WL] = both[half_lanes:]


def fit(low, main, high, rec, shift):
    comps, shots, width = main.shape
    rows = comps * (width // WL)
    span = 3 * LANES
    top = HALF + TAPS - 1 + 2 * LAG
    lanes_shift = jnp.tile(shift, LANES // shots)[None, :]
    vec = lambda n: pltpu.VMEM((n, rows, LANES), jnp.float32)
    return pl.pallas_call(
        fit_kernel,
        out_shape=jax.ShapeDtypeStruct(main.shape, jnp.float32),
        in_specs=[pl.BlockSpec(memory_space=pltpu.VMEM)] * 5,
        out_specs=pl.BlockSpec(memory_space=pltpu.VMEM),
        scratch_shapes=[
            pltpu.VMEM((rows * span, LANES), jnp.float32),
            vec(top),
            vec(top),
            pltpu.VMEM((rows * HALF, LANES), jnp.float32),
            pltpu.VMEM((TAPS, TAPS + 1, rows, LANES), jnp.float32),
            vec(TAPS),
        ],
        compiler_params=pltpu.CompilerParams(vmem_limit_bytes=32 * 1024 * 1024),
    )(low, main, high, rec, lanes_shift)


def product_kernel(order_ref, *refs, layout, has_base):
    panel_ref, out_ref, by_real, by_imag = refs[-4:]
    groups, comps, shots, width = out_ref.shape
    step = pl.program_id(1)
    real, imag = panel_ref[0], panel_ref[1]

    @pl.when(step == 0)
    def _():
        by_real[...] = jnp.zeros_like(by_real)
        by_imag[...] = jnp.zeros_like(by_imag)

    def add(pieces):
        flat = [piece[...].reshape(-1, piece.shape[-1]) for piece in pieces]
        rows = jnp.concatenate(flat, axis=0) if len(flat) > 1 else flat[0]
        by_real[...] += jnp.dot(rows, real, preferred_element_type=jnp.float32)
        by_imag[...] += jnp.dot(rows, imag, preferred_element_type=jnp.float32)

    at = 0
    for n, count in enumerate(layout):
        pieces = refs[at : at + count]
        at += count
        pl.when(step == n)(functools.partial(add, pieces))

    @pl.when(step == pl.num_programs(1) - 1)
    def _():
        for g in range(groups):
            row = 2 * g * shots
            real_part = by_real[row : row + shots] - by_imag[row + shots : row + 2 * shots]
            imag_part = by_imag[row : row + shots] + by_real[row + shots : row + 2 * shots]
            if has_base:
                real_part += refs[at][g, 0]
                imag_part += refs[at][g, 1]
            out_ref[g, 0] = real_part
            out_ref[g, 1] = imag_part


def products(pieces, order, panel, depth, base=None):
    _, comps, _, width = panel.shape
    parts = len(pieces)
    tile = width // 2
    shots = pieces[0][0].shape[2]
    groups = sum(piece.shape[0] for piece in pieces[0])
    rows = groups * comps * shots
    flat = [piece for part in pieces for piece in part]
    specs = []
    for at, part in enumerate(pieces):
        for piece in part:
            block = at if piece.shape[3] > depth else 0
            specs.append(
                pl.BlockSpec(piece.shape[:3] + (depth,), lambda n, k, o, block=block: (0, 0, 0, block))
            )
    out_spec = pl.BlockSpec((groups, comps, shots, tile), lambda n, k, o: (0, 0, 0, n))
    if base is not None:
        flat.append(base)
        specs.append(out_spec)
    grid_spec = pltpu.PrefetchScalarGridSpec(
        num_scalar_prefetch=1,
        grid=(width // tile, parts),
        in_specs=specs
        + [pl.BlockSpec((None, comps, depth, tile), lambda n, k, o: (0, 0, o[k], n))],
        out_specs=out_spec,
        scratch_shapes=[pltpu.VMEM((rows, tile), jnp.float32)] * 2,
    )
    return pl.pallas_call(
        functools.partial(
            product_kernel,
            layout=tuple(len(part) for part in pieces),
            has_base=base is not None,
        ),
        grid_spec=grid_spec,
        out_shape=jax.ShapeDtypeStruct((groups, comps, shots, width), jnp.float32),
        compiler_params=pltpu.CompilerParams(vmem_limit_bytes=52 * 1024 * 1024),
        cost_estimate=pl.CostEstimate(
            flops=4 * rows * depth * parts * width,
            bytes_accessed=4 * depth * parts * width,
            transcendentals=0,
        ),
    )(order, *flat, panel)


CODES = 32766.0
FINE = 256.0


def code_kernel(first_ref, second_ref, out_ref):
    comps, shots, width = first_ref.shape
    blocks = width // LANES
    for c in range(comps):
        rows = slice(c * shots, (c + 1) * shots)
        lane = lax.broadcasted_iota(jnp.int32, (shots, LANES), 1)
        peak = jnp.full((shots, LANES), 2.0**-100, jnp.float32)
        sums = []
        for b in range(blocks):
            at = slice(b * LANES, (b + 1) * LANES)
            value = first_ref[c, :, at] + second_ref[c, :, at]
            sums.append(value)
            most = jnp.max(jnp.abs(value), axis=1, keepdims=True)
            peak = jnp.where(lane == b, jnp.maximum(peak, most), peak)
        power = jnp.ceil(jnp.log2(peak) * FINE)
        scale = jnp.exp2(power * (-1.0 / FINE)) * CODES
        for b in range(blocks):
            at = slice(b * LANES, (b + 1) * LANES)
            code = jnp.round(sums[b] * scale[:, b : b + 1])
            code = jnp.clip(code, -32767.0, 32767.0)
            out_ref[rows, at] = code.astype(jnp.int32).astype(jnp.int16)
        out_ref[rows, width:] = power.astype(jnp.int32).astype(jnp.int16)


def coded(first, second):
    comps, shots, width = first.shape
    return pl.pallas_call(
        code_kernel,
        out_shape=jax.ShapeDtypeStruct((comps * shots, width + LANES), jnp.int16),
        in_specs=[pl.BlockSpec(memory_space=pltpu.VMEM)] * 2,
        out_specs=pl.BlockSpec(memory_space=pltpu.VMEM),
        compiler_params=pltpu.CompilerParams(vmem_limit_bytes=16 * 1024 * 1024),
    )(first, second)


def sum_kernel(first_ref, second_ref, *refs):
    codes = refs[:-3]
    out_ref, start_ref, end_ref = refs[-3:]
    comps, shots, width = first_ref.shape
    blocks = width // LANES
    for c in range(comps):
        rows = slice(c * shots, (c + 1) * shots)
        scales = []
        for code in codes:
            power = code[rows, width:].astype(jnp.int32).astype(jnp.float32)
            scales.append(jnp.exp2(power * (1.0 / FINE)) * (1.0 / CODES))
        for b in range(blocks):
            at = slice(b * LANES, (b + 1) * LANES)
            value = first_ref[c, :, at] + second_ref[c, :, at]
            for code, scale in zip(codes, scales):
                part = code[rows, at].astype(jnp.int32).astype(jnp.float32)
                value = value + part * scale[:, b : b + 1]
            out_ref[c, :, at] = value
            if b == 0:
                start_ref[c] = value
            if b == blocks - 1:
                end_ref[c] = value


def summed(first, second, codes):
    comps, shots, width = first.shape
    end = jax.ShapeDtypeStruct((comps, shots, LANES), jnp.float32)
    return pl.pallas_call(
        sum_kernel,
        out_shape=(jax.ShapeDtypeStruct(first.shape, jnp.float32), end, end),
        in_specs=[pl.BlockSpec(memory_space=pltpu.VMEM)] * (2 + len(codes)),
        out_specs=(pl.BlockSpec(memory_space=pltpu.VMEM),) * 3,
        compiler_params=pltpu.CompilerParams(vmem_limit_bytes=16 * 1024 * 1024),
    )(first, second, *codes)


def chosen(rows, aperture, panels):
    named = aperture.T[None] == panels[:, None, None]
    out = jnp.zeros((panels.shape[0],) + rows.shape[1:], rows.dtype)
    for a in range(rows.shape[0]):
        out = jnp.where(named[:, a, None, :, None], rows[a][None], out)
    return out


def predict_dense(shot_rows, aperture, panel):
    panel_count = lax.axis_size("shot")
    me = lax.axis_index("shot")
    parts = lax.axis_size("sec") * lax.axis_size("win")
    depth = shot_rows.shape[3] // parts
    part = lax.axis_index("sec") * lax.axis_size("win") + lax.axis_index("win")

    def partner(value, step):
        return lax.ppermute(value, "shot", [(i, i ^ step) for i in range(panel_count)])

    def across(value, axis):
        return lax.ppermute(value, axis, [(0, 1), (1, 0)])

    fence = lax.optimization_barrier
    order = jnp.bitwise_xor(part, jnp.arange(parts, dtype=jnp.int32))

    def turned(rows, n):
        here = lax.dynamic_slice_in_dim(rows, order[n] * depth, depth, 3)
        return here.transpose(1, 2, 0, 3)

    def panels(steps):
        return jnp.bitwise_xor(me, jnp.array(steps, jnp.int32))

    def exchange(far, steps):
        got = [partner(far[n : n + 1], k) for n, k in enumerate(steps)]
        return jnp.concatenate(got, axis=0)

    cut = 2 * ((panel_count + 2) // 4 + 1)
    early, late = list(range(2, cut)), list(range(cut, panel_count))
    mine = turned(shot_rows, 0)
    far = chosen(mine, aperture, panels(early + late))
    own = exchange(far, early)
    far, shot_rows, own = fence((far, shot_rows, own))
    by_sec, by_win = across(own, "sec"), across(own, "win")
    own_late = exchange(far[len(early) :], late)
    pieces = [turned(shot_rows, n) for n in range(parts)]
    local = [chosen(piece, aperture, panels([0, 1])) for piece in pieces]
    sibling = [partner(jnp.concatenate([piece[1:] for piece in local], axis=0), 1)]
    half = len(early) // 2
    both = (across(by_sec[:half], "win"), across(by_win[half:], "sec"))
    late_sec, late_win = across(own_late, "sec"), across(own_late, "win")
    exchanged = ((own,), (by_win,), (by_sec,), both)
    lists = [
        (local[n][:1], sibling[0][n : n + 1]) + tuple(exchanged[n]) for n in range(parts)
    ]
    terms = products(lists, order, panel, depth)
    late_sec, late_win, terms = fence((late_sec, late_win, terms))
    half = len(late) // 2
    late_both = (across(late_sec[:half], "win"), across(late_win[half:], "sec"))
    most = products(((own_late,), (late_win,), (late_sec,)), order[:3], panel, depth)
    others = [partner(terms[n + 1], 1) for n in range(0, 2 + len(early), 2)]
    codes = [coded(terms[2 * n], others[n]) for n in range(1, 1 + len(early) // 2)]
    late_both, codes, others = fence((late_both, codes, others))
    last = products((late_both,), order[3:], panel, depth, most)
    codes = [partner(code, k) for code, k in zip(codes, early[::2])]
    late_others = [partner(last[n + 1], 1) for n in range(0, len(late), 2)]
    late_others, codes = fence((late_others, codes))
    for n, k in enumerate(late[::2]):
        codes.append(partner(coded(last[2 * n], late_others[n]), k))
    return summed(terms[0], others[0], codes)


def predict_slots(shot_rows, aperture, panel, capacity):
    shot_count, slot_count = aperture.shape
    row_count = shot_count * slot_count
    trace_width = shot_rows.shape[3]
    recv_width = panel.shape[3]
    panel_count = lax.axis_size("shot")
    weights = panel[0]
    ap_flat = aperture.reshape(row_count)
    indicator = (ap_flat[:, None] == jnp.arange(panel_count, dtype=jnp.int32)[None, :]).astype(
        jnp.int32
    )
    earlier = jnp.cumsum(indicator, axis=0) - indicator
    position = jnp.sum(earlier * indicator, axis=1)
    slot_id = ap_flat * capacity + position
    source = (
        jnp.zeros((panel_count * capacity,), jnp.int32)
        .at[slot_id]
        .set(jnp.arange(row_count, dtype=jnp.int32))
    )
    rows_flat = shot_rows.reshape(row_count, 2, trace_width)
    outgoing = rows_flat[source].reshape(panel_count, capacity, 2, trace_width)
    received = lax.all_to_all(outgoing, "shot", split_axis=0, concat_axis=0, tiled=True)
    stacked = received.reshape(panel_count * capacity, 2, trace_width)
    parts = jnp.einsum("mck,dkr->mcdr", stacked, weights, preferred_element_type=jnp.float32)
    real_part = parts[:, 0, 0] - parts[:, 1, 1]
    imag_part = parts[:, 0, 1] + parts[:, 1, 0]
    terms = jnp.stack([real_part, imag_part], axis=1)
    terms = terms.reshape(panel_count, capacity, 2, recv_width)
    returned = lax.all_to_all(terms, "shot", split_axis=0, concat_axis=0, tiled=True)
    back_flat = returned.reshape(panel_count * capacity, 2, recv_width)
    predicted = jnp.sum(back_flat[slot_id].reshape(shot_count, slot_count, 2, recv_width), axis=1)
    return predicted.transpose(1, 0, 2)


def body(shot_rows, aperture, panel, recorded, shift):
    shot_count, slot_count = aperture.shape
    capacity = 2 * shot_count * slot_count // lax.axis_size("shot")
    columns = (lax.axis_size("sec"), lax.axis_size("win"))
    if capacity >= shot_count and lax.axis_size("shot") > 4 and columns == (2, 2):
        predicted, start, end = predict_dense(shot_rows, aperture, panel)
    else:
        predicted = predict_slots(shot_rows, aperture, panel, capacity)
        start, end = predicted[:, :, :LANES], predicted[:, :, -LANES:]
    count = lax.axis_size(("sec", "win"))
    forward = [(i, i + 1) for i in range(count - 1)]
    backward = [(target, source) for source, target in forward]
    low = lax.ppermute(end, ("sec", "win"), forward)
    high = lax.ppermute(start, ("sec", "win"), backward)
    primaries = fit(low, predicted, high, recorded.transpose(1, 0, 2), shift)
    return (predicted.transpose(1, 0, 2), primaries.transpose(1, 0, 2))


def solution(mesh):
    in_specs = (
        P("shot", None, None, None),
        P("shot", None),
        P("shot", None, None, ("sec", "win")),
        P("shot", None, ("sec", "win")),
        P("shot"),
    )
    out_specs = (P("shot", None, ("sec", "win")), P("shot", None, ("sec", "win")))
    return jax.shard_map(body, mesh=mesh, in_specs=in_specs, out_specs=out_specs, check_vma=False)
```

```python
import functools

import jax
import jax.numpy as jnp
from jax import lax
from jax.experimental import pallas as pl
from jax.experimental.pallas import tpu as pltpu
from jax.sharding import PartitionSpec as P

TAPS = 31
WL = 256
LAG = 8
EDGE = (TAPS - 1) // 2 + LAG
LANES = 128
HALF = WL // 2


def fit_kernel(low_ref, main_ref, high_ref, rec_ref, shift_ref, out_ref, piece, ext, raw, tgt, gram, res):
    comps, shots, width = main_ref.shape
    windows = width // WL
    span = 3 * LANES
    rows = comps * windows
    half_lanes = LANES // 2

    def block_of(c, b):
        if b == 0:
            return low_ref[c]
        if b == width // LANES + 1:
            return high_ref[c]
        return main_ref[c, :, (b - 1) * LANES : b * LANES]

    for c in range(comps):
        blocks = [block_of(c, b) for b in range(width // LANES + 2)]
        turned = [
            jnp.concatenate([blocks[b], blocks[b + 1]], axis=0).T for b in range(width // LANES + 1)
        ]
        for w in range(windows):
            g = c * windows + w
            for b in range(3):
                base = g * span + b * LANES
                piece[base : base + LANES, :] = turned[2 * w + b]
            pair = jnp.concatenate(
                [
                    rec_ref[c, :, w * WL : w * WL + HALF],
                    rec_ref[c, :, w * WL + HALF : (w + 1) * WL],
                ],
                axis=0,
            ).astype(jnp.float32)
            tgt[g * HALF : (g + 1) * HALF, :] = pair.T

    first = LANES - EDGE
    need = HALF + TAPS - 1
    top = need + 2 * LAG
    lag_of = jnp.broadcast_to(shift_ref[...], (rows, LANES))

    for i in range(top):
        raw[i] = piece[pl.ds(first + i, rows, stride=span), :]
    bit = [(lag_of & (1 << n)) != 0 for n in range(5)]
    count = need + 14
    for i in range(count):
        ext[i] = jnp.where(bit[0], raw[i + 1], raw[i])
    for n in range(1, 4):
        count -= 1 << n
        for i in range(count):
            ext[i] = jnp.where(bit[n], ext[i + (1 << n)], ext[i])
    for i in range(need):
        ext[i] = jnp.where(bit[4], raw[i + 16], ext[i])

    def total(v):
        v = v + pltpu.roll(v, rows // 2, 0)
        return v + pltpu.roll(v, half_lanes, 1)

    zero = jnp.zeros((rows, LANES), jnp.float32)
    unroll = 2

    def core(step, acc):
        i = TAPS - 1 + step * unroll
        vals = [ext[i + n] for n in range(TAPS + unroll - 1)]
        for n in range(unroll):
            acc = tuple(acc[d] + vals[n] * vals[n + d] for d in range(TAPS))
        return acc

    cores = lax.fori_loop(0, (HALF - TAPS + 1) // unroll, core, (zero,) * TAPS)
    for d in range(TAPS):
        last = TAPS - 1 - d
        run = cores[d]
        heads = [None] * (last + 1)
        if last == TAPS - 1:
            heads[last] = run
        for i in range(TAPS - 2, -1, -1):
            run = run + ext[i] * ext[i + d]
            if i <= last:
                heads[i] = run
        tail = zero
        for j in range(last + 1):
            if j > 0:
                tail = tail + ext[HALF + j - 1] * ext[HALF + j - 1 + d]
            value = total(heads[j] + tail)
            gram[j, j + d] = value + 1.0 if d == 0 else value

    def moments(step, acc):
        i = step * unroll
        vals = [ext[i + n] for n in range(TAPS + unroll - 1)]
        for n in range(unroll):
            row = tgt[pl.ds(i + n, rows, stride=HALF), :]
            acc = tuple(acc[j] + row * vals[n + j] for j in range(TAPS))
        return acc

    sums = lax.fori_loop(0, HALF // unroll, moments, (zero,) * TAPS)
    for j in range(TAPS):
        gram[j, TAPS] = total(sums[j])

    inverse = []
    for col in range(TAPS):
        rows_here = tuple(gram[col, r] for r in range(col, TAPS + 1))
        if col:

            def reduce(k, acc, col=col):
                mult = gram[k, col] * res[k]
                return tuple(acc[r - col] - mult * gram[k, r] for r in range(col, TAPS + 1))

            rows_here = lax.fori_loop(0, col, reduce, rows_here)
        for r in range(col, TAPS + 1):
            gram[col, r] = rows_here[r - col]
        res[col] = 1.0 / rows_here[0]

    left = [gram[k, TAPS] for k in range(TAPS)]
    taps = [None] * TAPS
    for r in range(TAPS - 1, -1, -1):
        taps[r] = left[r] * res[r]
        for k in range(r):
            left[k] = left[k] - gram[k, r] * taps[r]

    def subtract(step, carry):
        i = step * unroll
        vals = [ext[i + n] for n in range(TAPS + unroll - 1)]
        for n in range(unroll):
            value = tgt[pl.ds(i + n, rows, stride=HALF), :]
            fit = [zero, zero, zero, zero]
            for j in range(TAPS):
                fit[j % 4] = fit[j % 4] + carry[j] * vals[n + j]
            value = value - ((fit[0] + fit[1]) + (fit[2] + fit[3]))
            tgt[pl.ds(i + n, rows, stride=HALF), :] = value
        return carry

    lax.fori_loop(0, HALF // unroll, subtract, tuple(taps))
    for c in range(comps):
        for w in range(windows):
            g = c * windows + w
            both = tgt[g * HALF : (g + 1) * HALF, :].T
            out_ref[c, :, w * WL : w * WL + HALF] = both[:half_lanes]
            out_ref[c, :, w * WL + HALF : (w + 1) * WL] = both[half_lanes:]


def fit(low, main, high, rec, shift):
    comps, shots, width = main.shape
    rows = comps * (width // WL)
    span = 3 * LANES
    top = HALF + TAPS - 1 + 2 * LAG
    lanes_shift = jnp.tile(shift, LANES // shots)[None, :]
    vec = lambda n: pltpu.VMEM((n, rows, LANES), jnp.float32)
    return pl.pallas_call(
        fit_kernel,
        out_shape=jax.ShapeDtypeStruct(main.shape, jnp.float32),
        in_specs=[pl.BlockSpec(memory_space=pltpu.VMEM)] * 5,
        out_specs=pl.BlockSpec(memory_space=pltpu.VMEM),
        scratch_shapes=[
            pltpu.VMEM((rows * span, LANES), jnp.float32),
            vec(top),
            vec(top),
            pltpu.VMEM((rows * HALF, LANES), jnp.float32),
            pltpu.VMEM((TAPS, TAPS + 1, rows, LANES), jnp.float32),
            vec(TAPS),
        ],
        compiler_params=pltpu.CompilerParams(vmem_limit_bytes=32 * 1024 * 1024),
    )(low, main, high, rec, lanes_shift)


def product_kernel(order_ref, *refs, layout):
    panel_ref, keep_ref, swap_ref, by_real, by_imag = refs[-5:]
    pairs, comps, shots, width = keep_ref.shape
    step = pl.program_id(1)
    real, imag = panel_ref[0], panel_ref[1]

    @pl.when(step == 0)
    def _():
        by_real[...] = jnp.zeros_like(by_real)
        by_imag[...] = jnp.zeros_like(by_imag)

    def add(pieces):
        flat = [piece[...].reshape(-1, piece.shape[-1]) for piece in pieces]
        rows = jnp.concatenate(flat, axis=0) if len(flat) > 1 else flat[0]
        by_real[...] += jnp.dot(rows, real, preferred_element_type=jnp.float32)
        by_imag[...] += jnp.dot(rows, imag, preferred_element_type=jnp.float32)

    at = 0
    for n, count in enumerate(layout):
        pieces = refs[at : at + count]
        at += count
        pl.when(step == n)(functools.partial(add, pieces))

    @pl.when(step == pl.num_programs(1) - 1)
    def _():
        for g in range(2 * pairs):
            row = 2 * g * shots
            real_part = by_real[row : row + shots] - by_imag[row + shots : row + 2 * shots]
            imag_part = by_imag[row : row + shots] + by_real[row + shots : row + 2 * shots]
            out_ref = swap_ref if g % 2 else keep_ref
            out_ref[g // 2, 0] = real_part
            out_ref[g // 2, 1] = imag_part


def products(pieces, order, panel, depth):
    _, comps, _, width = panel.shape
    parts = len(pieces)
    tile = width // 2
    shots = pieces[0][0].shape[2]
    groups = sum(piece.shape[0] for piece in pieces[0])
    rows = groups * comps * shots
    flat = [piece for part in pieces for piece in part]
    specs = []
    for at, part in enumerate(pieces):
        for piece in part:
            block = at if piece.shape[3] > depth else 0
            specs.append(
                pl.BlockSpec(piece.shape[:3] + (depth,), lambda n, k, o, block=block: (0, 0, 0, block))
            )
    out_spec = pl.BlockSpec((groups // 2, comps, shots, tile), lambda n, k, o: (0, 0, 0, n))
    grid_spec = pltpu.PrefetchScalarGridSpec(
        num_scalar_prefetch=1,
        grid=(width // tile, parts),
        in_specs=specs
        + [pl.BlockSpec((None, comps, depth, tile), lambda n, k, o: (0, 0, o[k], n))],
        out_specs=(out_spec, out_spec),
        scratch_shapes=[pltpu.VMEM((rows, tile), jnp.float32)] * 2,
    )
    return pl.pallas_call(
        functools.partial(
            product_kernel,
            layout=tuple(len(part) for part in pieces),
        ),
        grid_spec=grid_spec,
        out_shape=(jax.ShapeDtypeStruct((groups // 2, comps, shots, width), jnp.float32),) * 2,
        compiler_params=pltpu.CompilerParams(vmem_limit_bytes=52 * 1024 * 1024),
        cost_estimate=pl.CostEstimate(
            flops=4 * rows * depth * parts * width,
            bytes_accessed=4 * depth * parts * width,
            transcendentals=0,
        ),
    )(order, *flat, panel)


CODES = 32766.0
FINE = 256.0


def code_kernel(first_ref, second_ref, out_ref):
    comps, shots, width = first_ref.shape
    blocks = width // LANES
    for c in range(comps):
        rows = slice(c * shots, (c + 1) * shots)
        lane = lax.broadcasted_iota(jnp.int32, (shots, LANES), 1)
        peak = jnp.full((shots, LANES), 2.0**-100, jnp.float32)
        sums = []
        for b in range(blocks):
            at = slice(b * LANES, (b + 1) * LANES)
            value = first_ref[c, :, at] + second_ref[c, :, at]
            sums.append(value)
            most = jnp.max(jnp.abs(value), axis=1, keepdims=True)
            peak = jnp.where(lane == b, jnp.maximum(peak, most), peak)
        power = jnp.ceil(jnp.log2(peak) * FINE)
        scale = jnp.exp2(power * (-1.0 / FINE)) * CODES
        for b in range(blocks):
            at = slice(b * LANES, (b + 1) * LANES)
            code = jnp.round(sums[b] * scale[:, b : b + 1])
            code = jnp.clip(code, -32767.0, 32767.0)
            out_ref[rows, at] = code.astype(jnp.int32).astype(jnp.int16)
        out_ref[rows, width:] = power.astype(jnp.int32).astype(jnp.int16)


def pair_spec(array, pair):
    return pl.BlockSpec((None,) + array.shape[1:], lambda i: (pair, 0, 0, 0))


def coded(first, second, pair):
    _, comps, shots, width = first.shape
    return pl.pallas_call(
        code_kernel,
        grid=(1,),
        out_shape=jax.ShapeDtypeStruct((comps * shots, width + LANES), jnp.int16),
        in_specs=[pair_spec(first, pair), pair_spec(second, pair)],
        out_specs=pl.BlockSpec((comps * shots, width + LANES), lambda i: (0, 0)),
        compiler_params=pltpu.CompilerParams(vmem_limit_bytes=16 * 1024 * 1024),
    )(first, second)


def sum_kernel(first_ref, second_ref, *refs):
    codes = refs[:-3]
    out_ref, start_ref, end_ref = refs[-3:]
    comps, shots, width = first_ref.shape
    blocks = width // LANES
    for c in range(comps):
        rows = slice(c * shots, (c + 1) * shots)
        scales = []
        for code in codes:
            power = code[rows, width:].astype(jnp.int32).astype(jnp.float32)
            scales.append(jnp.exp2(power * (1.0 / FINE)) * (1.0 / CODES))
        for b in range(blocks):
            at = slice(b * LANES, (b + 1) * LANES)
            value = first_ref[c, :, at] + second_ref[c, :, at]
            for code, scale in zip(codes, scales):
                part = code[rows, at].astype(jnp.int32).astype(jnp.float32)
                value = value + part * scale[:, b : b + 1]
            out_ref[c, :, at] = value
            if b == 0:
                start_ref[c] = value
            if b == blocks - 1:
                end_ref[c] = value


def summed(first, second, codes):
    _, comps, shots, width = first.shape
    end = jax.ShapeDtypeStruct((comps, shots, LANES), jnp.float32)
    return pl.pallas_call(
        sum_kernel,
        grid=(1,),
        out_shape=(jax.ShapeDtypeStruct(first.shape[1:], jnp.float32), end, end),
        in_specs=[pair_spec(first, 0), pair_spec(second, 0)]
        + [pl.BlockSpec(code.shape, lambda i: (0, 0)) for code in codes],
        out_specs=(pl.BlockSpec(first.shape[1:], lambda i: (0, 0, 0)),)
        + (pl.BlockSpec(end.shape, lambda i: (0, 0, 0)),) * 2,
        compiler_params=pltpu.CompilerParams(vmem_limit_bytes=16 * 1024 * 1024),
    )(first, second, *codes)


def chosen(rows, aperture, panels):
    named = aperture.T[None] == panels[:, None, None]
    out = jnp.zeros((panels.shape[0],) + rows.shape[1:], rows.dtype)
    for a in range(rows.shape[0]):
        out = jnp.where(named[:, a, None, :, None], rows[a][None], out)
    return out


def predict_dense(shot_rows, aperture, panel):
    panel_count = lax.axis_size("shot")
    me = lax.axis_index("shot")
    parts = lax.axis_size("sec") * lax.axis_size("win")
    depth = shot_rows.shape[3] // parts
    part = lax.axis_index("sec") * lax.axis_size("win") + lax.axis_index("win")

    def partner(value, step):
        return lax.ppermute(value, "shot", [(i, i ^ step) for i in range(panel_count)])

    def across(value, axis):
        return lax.ppermute(value, axis, [(0, 1), (1, 0)])

    fence = lax.optimization_barrier
    order = jnp.bitwise_xor(part, jnp.arange(parts, dtype=jnp.int32))

    def turned(rows, n):
        here = lax.dynamic_slice_in_dim(rows, order[n] * depth, depth, 3)
        return here.transpose(1, 2, 0, 3)

    def panels(steps):
        return jnp.bitwise_xor(me, jnp.array(steps, jnp.int32))

    def exchange(far, steps):
        got = [partner(far[n : n + 1], k) for n, k in enumerate(steps)]
        return jnp.concatenate(got, axis=0)

    cut = 2 * ((panel_count + 2) // 4 + 1)
    early, late = list(range(2, cut)), list(range(cut, panel_count))
    mine = turned(shot_rows, 0)
    far = chosen(mine, aperture, panels(early + late))
    own = exchange(far, early)
    far, shot_rows, own = fence((far, shot_rows, own))
    by_sec, by_win = across(own, "sec"), across(own, "win")
    own_late = exchange(far[len(early) :], late)
    pieces = [turned(shot_rows, n) for n in range(parts)]
    local = [chosen(piece, aperture, panels([0, 1])) for piece in pieces]
    sibling = [partner(jnp.concatenate([piece[1:] for piece in local], axis=0), 1)]
    half = len(early) // 2
    both = (across(by_sec[:half], "win"), across(by_win[half:], "sec"))
    late_sec, late_win = across(own_late, "sec"), across(own_late, "win")
    exchanged = ((own,), (by_win,), (by_sec,), both)
    lists = [
        (local[n][:1], sibling[0][n : n + 1]) + tuple(exchanged[n]) for n in range(parts)
    ]
    keep, swap = products(lists, order, panel, depth)
    late_sec, late_win, keep, swap = fence((late_sec, late_win, keep, swap))
    half = len(late) // 2
    late_both = (across(late_sec[:half], "win"), across(late_win[half:], "sec"))
    swap = partner(swap, 1)
    codes = [coded(keep, swap, n) for n in range(1, 1 + len(early) // 2)]
    late_both, codes, swap = fence((late_both, codes, swap))
    last, late_swap = products(
        ((own_late,), (late_win,), (late_sec,), late_both), order, panel, depth
    )
    codes = [partner(code, k) for code, k in zip(codes, early[::2])]
    late_swap, codes = fence((late_swap, codes))
    late_swap = partner(late_swap, 1)
    for n, k in enumerate(late[::2]):
        codes.append(partner(coded(last, late_swap, n), k))
    return summed(keep, swap, codes)


def predict_slots(shot_rows, aperture, panel, capacity):
    shot_count, slot_count = aperture.shape
    row_count = shot_count * slot_count
    trace_width = shot_rows.shape[3]
    recv_width = panel.shape[3]
    panel_count = lax.axis_size("shot")
    weights = panel[0]
    ap_flat = aperture.reshape(row_count)
    indicator = (ap_flat[:, None] == jnp.arange(panel_count, dtype=jnp.int32)[None, :]).astype(
        jnp.int32
    )
    earlier = jnp.cumsum(indicator, axis=0) - indicator
    position = jnp.sum(earlier * indicator, axis=1)
    slot_id = ap_flat * capacity + position
    source = (
        jnp.zeros((panel_count * capacity,), jnp.int32)
        .at[slot_id]
        .set(jnp.arange(row_count, dtype=jnp.int32))
    )
    rows_flat = shot_rows.reshape(row_count, 2, trace_width)
    outgoing = rows_flat[source].reshape(panel_count, capacity, 2, trace_width)
    received = lax.all_to_all(outgoing, "shot", split_axis=0, concat_axis=0, tiled=True)
    stacked = received.reshape(panel_count * capacity, 2, trace_width)
    parts = jnp.einsum("mck,dkr->mcdr", stacked, weights, preferred_element_type=jnp.float32)
    real_part = parts[:, 0, 0] - parts[:, 1, 1]
    imag_part = parts[:, 0, 1] + parts[:, 1, 0]
    terms = jnp.stack([real_part, imag_part], axis=1)
    terms = terms.reshape(panel_count, capacity, 2, recv_width)
    returned = lax.all_to_all(terms, "shot", split_axis=0, concat_axis=0, tiled=True)
    back_flat = returned.reshape(panel_count * capacity, 2, recv_width)
    predicted = jnp.sum(back_flat[slot_id].reshape(shot_count, slot_count, 2, recv_width), axis=1)
    return predicted.transpose(1, 0, 2)


def body(shot_rows, aperture, panel, recorded, shift):
    shot_count, slot_count = aperture.shape
    capacity = 2 * shot_count * slot_count // lax.axis_size("shot")
    columns = (lax.axis_size("sec"), lax.axis_size("win"))
    if capacity >= shot_count and lax.axis_size("shot") > 4 and columns == (2, 2):
        predicted, start, end = predict_dense(shot_rows, aperture, panel)
    else:
        predicted = predict_slots(shot_rows, aperture, panel, capacity)
        start, end = predicted[:, :, :LANES], predicted[:, :, -LANES:]
    count = lax.axis_size(("sec", "win"))
    forward = [(i, i + 1) for i in range(count - 1)]
    backward = [(target, source) for source, target in forward]
    low = lax.ppermute(end, ("sec", "win"), forward)
    high = lax.ppermute(start, ("sec", "win"), backward)
    primaries = fit(low, predicted, high, recorded.transpose(1, 0, 2), shift)
    return (predicted.transpose(1, 0, 2), primaries.transpose(1, 0, 2))


def solution(mesh):
    in_specs = (
        P("shot", None, None, None),
        P("shot", None),
        P("shot", None, None, ("sec", "win")),
        P("shot", None, ("sec", "win")),
        P("shot"),
    )
    out_specs = (P("shot", None, ("sec", "win")), P("shot", None, ("sec", "win")))
    return jax.shard_map(body, mesh=mesh, in_specs=in_specs, out_specs=out_specs, check_vma=False)
```

```python
import functools

import jax
import jax.numpy as jnp
from jax import lax
from jax.experimental import pallas as pl
from jax.experimental.pallas import tpu as pltpu
from jax.sharding import PartitionSpec as P

TAPS = 31
WL = 256
LAG = 8
EDGE = (TAPS - 1) // 2 + LAG
LANES = 128
HALF = WL // 2


def fit_kernel(low_ref, main_ref, high_ref, rec_ref, shift_ref, out_ref, piece, ext, raw, tgt, gram, res):
    comps, shots, width = main_ref.shape
    windows = width // WL
    span = 3 * LANES
    rows = comps * windows
    half_lanes = LANES // 2

    def block_of(c, b):
        if b == 0:
            return low_ref[c]
        if b == width // LANES + 1:
            return high_ref[c]
        return main_ref[c, :, (b - 1) * LANES : b * LANES]

    for c in range(comps):
        blocks = [block_of(c, b) for b in range(width // LANES + 2)]
        turned = [
            jnp.concatenate([blocks[b], blocks[b + 1]], axis=0).T for b in range(width // LANES + 1)
        ]
        for w in range(windows):
            g = c * windows + w
            for b in range(3):
                base = g * span + b * LANES
                piece[base : base + LANES, :] = turned[2 * w + b]
            pair = jnp.concatenate(
                [
                    rec_ref[c, :, w * WL : w * WL + HALF],
                    rec_ref[c, :, w * WL + HALF : (w + 1) * WL],
                ],
                axis=0,
            ).astype(jnp.float32)
            tgt[g * HALF : (g + 1) * HALF, :] = pair.T

    first = LANES - EDGE
    need = HALF + TAPS - 1
    top = need + 2 * LAG
    lag_of = jnp.broadcast_to(shift_ref[...], (rows, LANES))

    for i in range(top):
        raw[i] = piece[pl.ds(first + i, rows, stride=span), :]
    bit = [(lag_of & (1 << n)) != 0 for n in range(5)]
    count = need + 14
    for i in range(count):
        ext[i] = jnp.where(bit[0], raw[i + 1], raw[i])
    for n in range(1, 4):
        count -= 1 << n
        for i in range(count):
            ext[i] = jnp.where(bit[n], ext[i + (1 << n)], ext[i])
    for i in range(need):
        ext[i] = jnp.where(bit[4], raw[i + 16], ext[i])

    def total(v):
        v = v + pltpu.roll(v, rows // 2, 0)
        return v + pltpu.roll(v, half_lanes, 1)

    zero = jnp.zeros((rows, LANES), jnp.float32)
    unroll = 2

    def core(step, acc):
        i = TAPS - 1 + step * unroll
        vals = [ext[i + n] for n in range(TAPS + unroll - 1)]
        for n in range(unroll):
            acc = tuple(acc[d] + vals[n] * vals[n + d] for d in range(TAPS))
        return acc

    cores = lax.fori_loop(0, (HALF - TAPS + 1) // unroll, core, (zero,) * TAPS)
    for d in range(TAPS):
        last = TAPS - 1 - d
        run = cores[d]
        heads = [None] * (last + 1)
        if last == TAPS - 1:
            heads[last] = run
        for i in range(TAPS - 2, -1, -1):
            run = run + ext[i] * ext[i + d]
            if i <= last:
                heads[i] = run
        tail = zero
        for j in range(last + 1):
            if j > 0:
                tail = tail + ext[HALF + j - 1] * ext[HALF + j - 1 + d]
            value = total(heads[j] + tail)
            gram[j, j + d] = value + 1.0 if d == 0 else value

    def moments(step, acc):
        i = step * unroll
        vals = [ext[i + n] for n in range(TAPS + unroll - 1)]
        for n in range(unroll):
            row = tgt[pl.ds(i + n, rows, stride=HALF), :]
            acc = tuple(acc[j] + row * vals[n + j] for j in range(TAPS))
        return acc

    sums = lax.fori_loop(0, HALF // unroll, moments, (zero,) * TAPS)
    for j in range(TAPS):
        gram[j, TAPS] = total(sums[j])

    inverse = []
    for col in range(TAPS):
        rows_here = tuple(gram[col, r] for r in range(col, TAPS + 1))
        if col:

            def reduce(k, acc, col=col):
                mult = gram[k, col] * res[k]
                return tuple(acc[r - col] - mult * gram[k, r] for r in range(col, TAPS + 1))

            def reduce_some(step, acc, reduce=reduce):
                for n in range(4):
                    acc = reduce(step * 4 + n, acc)
                return acc

            rows_here = lax.fori_loop(0, col // 4, reduce_some, rows_here)
            for k in range(col // 4 * 4, col):
                rows_here = reduce(k, rows_here)
        for r in range(col, TAPS + 1):
            gram[col, r] = rows_here[r - col]
        res[col] = 1.0 / rows_here[0]

    left = [gram[k, TAPS] for k in range(TAPS)]
    taps = [None] * TAPS
    for r in range(TAPS - 1, -1, -1):
        taps[r] = left[r] * res[r]
        for k in range(r):
            left[k] = left[k] - gram[k, r] * taps[r]

    def subtract(step, carry):
        i = step * unroll
        vals = [ext[i + n] for n in range(TAPS + unroll - 1)]
        for n in range(unroll):
            value = tgt[pl.ds(i + n, rows, stride=HALF), :]
            fit = [zero, zero, zero, zero]
            for j in range(TAPS):
                fit[j % 4] = fit[j % 4] + carry[j] * vals[n + j]
            value = value - ((fit[0] + fit[1]) + (fit[2] + fit[3]))
            tgt[pl.ds(i + n, rows, stride=HALF), :] = value
        return carry

    lax.fori_loop(0, HALF // unroll, subtract, tuple(taps))
    for c in range(comps):
        for w in range(windows):
            g = c * windows + w
            both = tgt[g * HALF : (g + 1) * HALF, :].T
            out_ref[c, :, w * WL : w * WL + HALF] = both[:half_lanes]
            out_ref[c, :, w * WL + HALF : (w + 1) * WL] = both[half_lanes:]


def fit(low, main, high, rec, shift):
    comps, shots, width = main.shape
    rows = comps * (width // WL)
    span = 3 * LANES
    top = HALF + TAPS - 1 + 2 * LAG
    lanes_shift = jnp.tile(shift, LANES // shots)[None, :]
    vec = lambda n: pltpu.VMEM((n, rows, LANES), jnp.float32)
    return pl.pallas_call(
        fit_kernel,
        out_shape=jax.ShapeDtypeStruct(main.shape, jnp.float32),
        in_specs=[pl.BlockSpec(memory_space=pltpu.VMEM)] * 5,
        out_specs=pl.BlockSpec(memory_space=pltpu.VMEM),
        scratch_shapes=[
            pltpu.VMEM((rows * span, LANES), jnp.float32),
            vec(top),
            vec(top),
            pltpu.VMEM((rows * HALF, LANES), jnp.float32),
            pltpu.VMEM((TAPS, TAPS + 1, rows, LANES), jnp.float32),
            vec(TAPS),
        ],
        compiler_params=pltpu.CompilerParams(vmem_limit_bytes=32 * 1024 * 1024),
    )(low, main, high, rec, lanes_shift)


def product_kernel(order_ref, *refs, layout):
    panel_ref, keep_ref, swap_ref, by_real, by_imag = refs[-5:]
    pairs, comps, shots, width = keep_ref.shape
    step = pl.program_id(1)
    real, imag = panel_ref[0], panel_ref[1]

    @pl.when(step == 0)
    def _():
        by_real[...] = jnp.zeros_like(by_real)
        by_imag[...] = jnp.zeros_like(by_imag)

    def add(pieces):
        flat = [piece[...].reshape(-1, piece.shape[-1]) for piece in pieces]
        rows = jnp.concatenate(flat, axis=0) if len(flat) > 1 else flat[0]
        by_real[...] += jnp.dot(rows, real, preferred_element_type=jnp.float32)
        by_imag[...] += jnp.dot(rows, imag, preferred_element_type=jnp.float32)

    at = 0
    for n, count in enumerate(layout):
        pieces = refs[at : at + count]
        at += count
        pl.when(step == n)(functools.partial(add, pieces))

    @pl.when(step == pl.num_programs(1) - 1)
    def _():
        for g in range(2 * pairs):
            row = 2 * g * shots
            real_part = by_real[row : row + shots] - by_imag[row + shots : row + 2 * shots]
            imag_part = by_imag[row : row + shots] + by_real[row + shots : row + 2 * shots]
            out_ref = swap_ref if g % 2 else keep_ref
            out_ref[g // 2, 0] = real_part
            out_ref[g // 2, 1] = imag_part


def products(pieces, order, panel, depth):
    _, comps, _, width = panel.shape
    parts = len(pieces)
    tile = width // 2
    shots = pieces[0][0].shape[2]
    groups = sum(piece.shape[0] for piece in pieces[0])
    rows = groups * comps * shots
    flat = [piece for part in pieces for piece in part]
    specs = []
    for at, part in enumerate(pieces):
        for piece in part:
            block = at if piece.shape[3] > depth else 0
            specs.append(
                pl.BlockSpec(piece.shape[:3] + (depth,), lambda n, k, o, block=block: (0, 0, 0, block))
            )
    out_spec = pl.BlockSpec((groups // 2, comps, shots, tile), lambda n, k, o: (0, 0, 0, n))
    grid_spec = pltpu.PrefetchScalarGridSpec(
        num_scalar_prefetch=1,
        grid=(width // tile, parts),
        in_specs=specs
        + [pl.BlockSpec((None, comps, depth, tile), lambda n, k, o: (0, 0, o[k], n))],
        out_specs=(out_spec, out_spec),
        scratch_shapes=[pltpu.VMEM((rows, tile), jnp.float32)] * 2,
    )
    return pl.pallas_call(
        functools.partial(
            product_kernel,
            layout=tuple(len(part) for part in pieces),
        ),
        grid_spec=grid_spec,
        out_shape=(jax.ShapeDtypeStruct((groups // 2, comps, shots, width), jnp.float32),) * 2,
        compiler_params=pltpu.CompilerParams(vmem_limit_bytes=52 * 1024 * 1024),
        cost_estimate=pl.CostEstimate(
            flops=4 * rows * depth * parts * width,
            bytes_accessed=4 * depth * parts * width,
            transcendentals=0,
        ),
    )(order, *flat, panel)


CODES = 32766.0
FINE = 256.0


def code_kernel(first_ref, second_ref, out_ref):
    comps, shots, width = first_ref.shape
    blocks = width // LANES
    for c in range(comps):
        rows = slice(c * shots, (c + 1) * shots)
        lane = lax.broadcasted_iota(jnp.int32, (shots, LANES), 1)
        peak = jnp.full((shots, LANES), 2.0**-100, jnp.float32)
        sums = []
        for b in range(blocks):
            at = slice(b * LANES, (b + 1) * LANES)
            value = first_ref[c, :, at] + second_ref[c, :, at]
            sums.append(value)
            most = jnp.max(jnp.abs(value), axis=1, keepdims=True)
            peak = jnp.where(lane == b, jnp.maximum(peak, most), peak)
        power = jnp.ceil(jnp.log2(peak) * FINE)
        scale = jnp.exp2(power * (-1.0 / FINE)) * CODES
        for b in range(blocks):
            at = slice(b * LANES, (b + 1) * LANES)
            code = jnp.round(sums[b] * scale[:, b : b + 1])
            code = jnp.clip(code, -32767.0, 32767.0)
            out_ref[rows, at] = code.astype(jnp.int32).astype(jnp.int16)
        out_ref[rows, width:] = power.astype(jnp.int32).astype(jnp.int16)


def pair_spec(array, pair):
    return pl.BlockSpec((None,) + array.shape[1:], lambda i: (pair, 0, 0, 0))


def coded(first, second, pair):
    _, comps, shots, width = first.shape
    return pl.pallas_call(
        code_kernel,
        grid=(1,),
        out_shape=jax.ShapeDtypeStruct((comps * shots, width + LANES), jnp.int16),
        in_specs=[pair_spec(first, pair), pair_spec(second, pair)],
        out_specs=pl.BlockSpec((comps * shots, width + LANES), lambda i: (0, 0)),
        compiler_params=pltpu.CompilerParams(vmem_limit_bytes=16 * 1024 * 1024),
    )(first, second)


def sum_kernel(first_ref, second_ref, *refs):
    codes = refs[:-3]
    out_ref, start_ref, end_ref = refs[-3:]
    comps, shots, width = first_ref.shape
    blocks = width // LANES
    for c in range(comps):
        rows = slice(c * shots, (c + 1) * shots)
        scales = []
        for code in codes:
            power = code[rows, width:].astype(jnp.int32).astype(jnp.float32)
            scales.append(jnp.exp2(power * (1.0 / FINE)) * (1.0 / CODES))
        for b in range(blocks):
            at = slice(b * LANES, (b + 1) * LANES)
            value = first_ref[c, :, at] + second_ref[c, :, at]
            for code, scale in zip(codes, scales):
                part = code[rows, at].astype(jnp.int32).astype(jnp.float32)
                value = value + part * scale[:, b : b + 1]
            out_ref[c, :, at] = value
            if b == 0:
                start_ref[c] = value
            if b == blocks - 1:
                end_ref[c] = value


def summed(first, second, codes):
    _, comps, shots, width = first.shape
    end = jax.ShapeDtypeStruct((comps, shots, LANES), jnp.float32)
    return pl.pallas_call(
        sum_kernel,
        grid=(1,),
        out_shape=(jax.ShapeDtypeStruct(first.shape[1:], jnp.float32), end, end),
        in_specs=[pair_spec(first, 0), pair_spec(second, 0)]
        + [pl.BlockSpec(code.shape, lambda i: (0, 0)) for code in codes],
        out_specs=(pl.BlockSpec(first.shape[1:], lambda i: (0, 0, 0)),)
        + (pl.BlockSpec(end.shape, lambda i: (0, 0, 0)),) * 2,
        compiler_params=pltpu.CompilerParams(vmem_limit_bytes=16 * 1024 * 1024),
    )(first, second, *codes)


def chosen(rows, aperture, panels):
    named = aperture.T[None] == panels[:, None, None]
    out = jnp.zeros((panels.shape[0],) + rows.shape[1:], rows.dtype)
    for a in range(rows.shape[0]):
        out = jnp.where(named[:, a, None, :, None], rows[a][None], out)
    return out


def predict_dense(shot_rows, aperture, panel):
    panel_count = lax.axis_size("shot")
    me = lax.axis_index("shot")
    parts = lax.axis_size("sec") * lax.axis_size("win")
    depth = shot_rows.shape[3] // parts
    part = lax.axis_index("sec") * lax.axis_size("win") + lax.axis_index("win")

    def partner(value, step):
        return lax.ppermute(value, "shot", [(i, i ^ step) for i in range(panel_count)])

    def across(value, axis):
        return lax.ppermute(value, axis, [(0, 1), (1, 0)])

    fence = lax.optimization_barrier
    order = jnp.bitwise_xor(part, jnp.arange(parts, dtype=jnp.int32))

    def turned(rows, n):
        here = lax.dynamic_slice_in_dim(rows, order[n] * depth, depth, 3)
        return here.transpose(1, 2, 0, 3)

    def panels(steps):
        return jnp.bitwise_xor(me, jnp.array(steps, jnp.int32))

    def exchange(far, steps):
        got = [partner(far[n : n + 1], k) for n, k in enumerate(steps)]
        return jnp.concatenate(got, axis=0)

    cut = 2 * ((panel_count + 2) // 4 + 1)
    early, late = list(range(2, cut)), list(range(cut, panel_count))
    mine = turned(shot_rows, 0)
    far = chosen(mine, aperture, panels(early + late))
    own = exchange(far, early)
    far, shot_rows, own = fence((far, shot_rows, own))
    by_sec, by_win = across(own, "sec"), across(own, "win")
    own_late = exchange(far[len(early) :], late)
    pieces = [turned(shot_rows, n) for n in range(parts)]
    local = [chosen(piece, aperture, panels([0, 1])) for piece in pieces]
    sibling = [partner(jnp.concatenate([piece[1:] for piece in local], axis=0), 1)]
    half = len(early) // 2
    both = (across(by_sec[:half], "win"), across(by_win[half:], "sec"))
    late_sec, late_win = across(own_late, "sec"), across(own_late, "win")
    exchanged = ((own,), (by_win,), (by_sec,), both)
    lists = [
        (local[n][:1], sibling[0][n : n + 1]) + tuple(exchanged[n]) for n in range(parts)
    ]
    keep, swap = products(lists, order, panel, depth)
    late_sec, late_win, keep, swap = fence((late_sec, late_win, keep, swap))
    half = len(late) // 2
    late_both = (across(late_sec[:half], "win"), across(late_win[half:], "sec"))
    swap = partner(swap, 1)
    codes = [coded(keep, swap, n) for n in range(1, 1 + len(early) // 2)]
    late_both, codes, swap = fence((late_both, codes, swap))
    last, late_swap = products(
        ((own_late,), (late_win,), (late_sec,), late_both), order, panel, depth
    )
    codes = [partner(code, k) for code, k in zip(codes, early[::2])]
    late_swap, codes = fence((late_swap, codes))
    late_swap = partner(late_swap, 1)
    for n, k in enumerate(late[::2]):
        codes.append(partner(coded(last, late_swap, n), k))
    return summed(keep, swap, codes)


def predict_slots(shot_rows, aperture, panel, capacity):
    shot_count, slot_count = aperture.shape
    row_count = shot_count * slot_count
    trace_width = shot_rows.shape[3]
    recv_width = panel.shape[3]
    panel_count = lax.axis_size("shot")
    weights = panel[0]
    ap_flat = aperture.reshape(row_count)
    indicator = (ap_flat[:, None] == jnp.arange(panel_count, dtype=jnp.int32)[None, :]).astype(
        jnp.int32
    )
    earlier = jnp.cumsum(indicator, axis=0) - indicator
    position = jnp.sum(earlier * indicator, axis=1)
    slot_id = ap_flat * capacity + position
    source = (
        jnp.zeros((panel_count * capacity,), jnp.int32)
        .at[slot_id]
        .set(jnp.arange(row_count, dtype=jnp.int32))
    )
    rows_flat = shot_rows.reshape(row_count, 2, trace_width)
    outgoing = rows_flat[source].reshape(panel_count, capacity, 2, trace_width)
    received = lax.all_to_all(outgoing, "shot", split_axis=0, concat_axis=0, tiled=True)
    stacked = received.reshape(panel_count * capacity, 2, trace_width)
    parts = jnp.einsum("mck,dkr->mcdr", stacked, weights, preferred_element_type=jnp.float32)
    real_part = parts[:, 0, 0] - parts[:, 1, 1]
    imag_part = parts[:, 0, 1] + parts[:, 1, 0]
    terms = jnp.stack([real_part, imag_part], axis=1)
    terms = terms.reshape(panel_count, capacity, 2, recv_width)
    returned = lax.all_to_all(terms, "shot", split_axis=0, concat_axis=0, tiled=True)
    back_flat = returned.reshape(panel_count * capacity, 2, recv_width)
    predicted = jnp.sum(back_flat[slot_id].reshape(shot_count, slot_count, 2, recv_width), axis=1)
    return predicted.transpose(1, 0, 2)


def body(shot_rows, aperture, panel, recorded, shift):
    shot_count, slot_count = aperture.shape
    capacity = 2 * shot_count * slot_count // lax.axis_size("shot")
    columns = (lax.axis_size("sec"), lax.axis_size("win"))
    if capacity >= shot_count and lax.axis_size("shot") > 4 and columns == (2, 2):
        predicted, start, end = predict_dense(shot_rows, aperture, panel)
    else:
        predicted = predict_slots(shot_rows, aperture, panel, capacity)
        start, end = predicted[:, :, :LANES], predicted[:, :, -LANES:]
    count = lax.axis_size(("sec", "win"))
    forward = [(i, i + 1) for i in range(count - 1)]
    backward = [(target, source) for source, target in forward]
    low = lax.ppermute(end, ("sec", "win"), forward)
    high = lax.ppermute(start, ("sec", "win"), backward)
    primaries = fit(low, predicted, high, recorded.transpose(1, 0, 2), shift)
    return (predicted.transpose(1, 0, 2), primaries.transpose(1, 0, 2))


def solution(mesh):
    in_specs = (
        P("shot", None, None, None),
        P("shot", None),
        P("shot", None, None, ("sec", "win")),
        P("shot", None, ("sec", "win")),
        P("shot"),
    )
    out_specs = (P("shot", None, ("sec", "win")), P("shot", None, ("sec", "win")))
    return jax.shard_map(body, mesh=mesh, in_specs=in_specs, out_specs=out_specs, check_vma=False)
```
